32 devices in a mesh: ax: 8 (over z, core), xs: 4 (over y, x).
Axes of the slice: x: 2, y: 2, z: 4, core: 2. Of those that a mesh axis runs over, the one named last changes fastest.
Arguments:
- scalar: float32 [64, 256, 1024], P('ax', 'xs'), may hold values from 0 to 1
- axial_rate: float32 [64, 256, 1024], P('ax', 'xs'), may hold values from 1.1 to 2.4
- swirl_rate: float32 [64, 256, 1024], P('ax', 'xs'), may hold values from -4 to 4
Outputs:
- transported: float32 [64, 256, 1024], P('ax', 'xs')
The draws below stay inside these ranges and needn't reach their ends.
All inputs are finite; a program needn't handle non-finite values.
Results may differ from the reference program's by a relative error of at most 0.00014.
Values sent between devices are 32-bit elements; how exact they have to be, the bound alone decides.
A program may use at most 64 MiB of HBM per device.

```python
import math
import jax
import jax.numpy as jnp
from jax import lax

NR = 256
NT = 1024
CZ = 8
SUBSTEPS = 2
NZ = 64


def block_levels(stream_key, dims, shards, least, top_value):
    loudness = 1.0
    for dim, blocks in shards:
        draws = jax.random.uniform(jax.random.fold_in(jax.random.fold_in(stream_key, 6), dim), (blocks,), jnp.float32, least / len(shards), top_value / len(shards))
        loudness = loudness * jnp.repeat(jnp.exp(draws), dims[dim] // blocks).reshape((-1,) + (1,) * (len(dims) - 1 - dim))
    return loudness


def normal_values(rng, extent, deviation, most, pieces=(), kind=jnp.bfloat16):
    values = deviation * jax.random.normal(rng, extent, jnp.float32)
    if pieces:
        values = values * block_levels(rng, extent, pieces, -0.22, 0.18)
    return jnp.clip(values, -most, most).astype(kind)


def setup_inputs(seed: int = 0) -> dict:
    streams_of = jax.random.split(jax.random.key(seed), 4)
    scalar = jnp.clip(1.0 * jax.random.uniform(streams_of[0], (NZ, NR, NT), jnp.float32) ** block_levels(streams_of[0], (NZ, NR, NT), ((0, 8), (1, 4)), -0.2, 0.2), 0.0, 1.0)
    axial_rate = jnp.clip(jnp.exp(math.log(2.4) - 0.7801586 * jax.random.uniform(streams_of[1], (NZ, NR, NT), jnp.float32) ** block_levels(streams_of[1], (NZ, NR, NT), ((0, 8), (1, 4)), -0.2, 0.2)), 1.1, 2.4)
    swirl_rate = normal_values(streams_of[2], (NZ, NR, NT), 1.0, 4.0, ((0, 8), (1, 4)), jnp.float32)
    return {"scalar": scalar, "axial_rate": axial_rate, "swirl_rate": swirl_rate}


axial_weight = 0.2
azimuth_damp = 0.5
diffusion_number = 1.0
stencil_coeffs = (-1.0 / 560.0, 8.0 / 315.0, -0.2, 1.6, -205.0 / 72.0, 1.6, -0.2, 8.0 / 315.0, -1.0 / 560.0)

def radial_bands(cell_count, diffusion_value):
    cell_index = jnp.arange(cell_count, dtype=jnp.float32)
    radius = cell_index + 0.5
    upper_face = jnp.where(cell_index < cell_count - 1, cell_index + 1.0, 0.0)
    sub_diag = -diffusion_value * cell_index / radius
    super_diag = -diffusion_value * upper_face / radius
    main_diag = 1.0 - sub_diag - super_diag
    return (sub_diag, main_diag, super_diag)

def reference(scalar, axial_rate, swirl_rate):
    sub_diag, main_diag, super_diag = radial_bands(NR, diffusion_number)
    band_shape = (NZ, NR)
    sub_full = jnp.broadcast_to(sub_diag, band_shape)
    main_full = jnp.broadcast_to(main_diag, band_shape)
    super_full = jnp.broadcast_to(super_diag, band_shape)
    radius = jnp.arange(NR, dtype=jnp.float32) + 0.5
    nyquist = NT // 2
    wavenum = jnp.arange(nyquist + 1, dtype=jnp.float32)
    damping = 1.0 / (1.0 + azimuth_damp * jnp.square(wavenum)[None, :] / jnp.square(radius)[:, None])
    slope_rate = jnp.where(wavenum < nyquist, wavenum * (2.0 * math.pi / NT), 0.0)
    courant = CZ * axial_rate
    factor = courant / (1.0 + courant)
    field_now = scalar
    for substep in range(SUBSTEPS):
        padded = jnp.pad(field_now, ((4, 4), (0, 0), (0, 0)))
        stencil_sum = jnp.zeros_like(field_now)
        for offset in range(9):
            stencil_sum = stencil_sum + stencil_coeffs[offset] * padded[offset:offset + NZ]
        explicit_field = field_now + axial_weight * stencil_sum
        solved = lax.linalg.tridiagonal_solve(sub_full, main_full, super_full, explicit_field)
        spectrum = jnp.fft.rfft(solved, axis=2) * damping
        smooth = jnp.fft.irfft(spectrum, n=NT, axis=2)
        azimuth_slope = jnp.fft.irfft(1j * slope_rate * spectrum, n=NT, axis=2)
        source = smooth - swirl_rate * azimuth_slope
        scaled = source / (1.0 + courant)

        def advance(carried, plane_pair):
            updated = plane_pair[0] * carried + plane_pair[1]
            return (updated, updated)
        final_value, field_now = lax.scan(advance, jnp.zeros((NR, NT), dtype=jnp.float32), (factor, scaled))
    return field_now
```

```python
import functools
import math

import jax
import jax.numpy as jnp
import ml_dtypes
import numpy as np
from jax import lax
from jax.experimental import pallas as pl
from jax.experimental.pallas import tpu as pltpu
from jax.sharding import PartitionSpec as P

CZ = 8
SUBSTEPS = 2
HALO = 4
CHUNK = 16
MESH = pl.DeviceIdType.MESH

axial_weight = 0.2
azimuth_damp = 0.5
diffusion_number = 1.0
stencil_coeffs = (
    -205.0 / 72.0,
    1.6,
    -0.2,
    8.0 / 315.0,
    -1.0 / 560.0,
)


def split_table(table):
    high = table.astype(np.float32).astype(ml_dtypes.bfloat16)
    low = (table - high.astype(np.float64)).astype(np.float32).astype(ml_dtypes.bfloat16)
    return high, low


def radial_tables(cells, groups):
    rows = cells // groups
    index = np.arange(cells, dtype=np.float64)
    radius = index + 0.5
    upper = np.where(index < cells - 1, index + 1.0, 0.0)
    sub = -diffusion_number * index / radius
    sup = -diffusion_number * upper / radius
    full = np.diag(1.0 - sub - sup) + np.diag(sub[1:], -1) + np.diag(sup[:-1], 1)
    local = np.zeros((groups, rows, rows))
    spikes = np.zeros((groups, rows, 2))
    coupling = np.zeros((2 * groups, 2 * groups))
    for d in range(groups):
        first, last = d * rows, (d + 1) * rows - 1
        local[d] = np.linalg.inv(full[first : last + 1, first : last + 1])
        if d > 0:
            spikes[d, :, 0] = -local[d][:, 0] * sub[first]
            coupling[2 * d, 2 * d - 1] = spikes[d, 0, 0]
            coupling[2 * d + 1, 2 * d - 1] = spikes[d, -1, 0]
        if d < groups - 1:
            spikes[d, :, 1] = -local[d][:, -1] * sup[last]
            coupling[2 * d, 2 * d + 2] = spikes[d, 0, 1]
            coupling[2 * d + 1, 2 * d + 2] = spikes[d, -1, 1]
    reduced = np.linalg.inv(np.eye(2 * groups) - coupling)
    mix = np.zeros((groups, 2, 2 * groups))
    for d in range(groups):
        if d > 0:
            mix[d, 0] = reduced[2 * d - 1]
        if d < groups - 1:
            mix[d, 1] = reduced[2 * d + 2]
    return local, spikes, mix


def azimuth_tables(points, cells, groups):
    half, quarter = points // 2, points // 4
    grid = np.arange(half)
    even, odd = 2 * np.arange(quarter), 2 * np.arange(quarter) + 1

    def angle(m):
        return (grid[:, None] * m[None, :] % points) * (2.0 * math.pi / points)

    sine_even = np.sin(angle(even))
    sine_even[:, 0] = np.cos(math.pi * grid)
    table_even = np.concatenate([np.cos(angle(even)), sine_even], axis=1)
    table_odd = np.concatenate([np.cos(angle(odd)), np.sin(angle(odd))], axis=1)
    sine_m = even.copy()
    sine_m[0] = half
    wave = np.concatenate([even, sine_m, odd, odd]).astype(np.float64)
    weight = np.where((wave == 0) | (wave == half), 1.0, 2.0) / points
    radius = np.arange(cells) + 0.5
    damp = weight / (1.0 + azimuth_damp * wave[None, :] ** 2 / radius[:, None] ** 2)
    rate_even = np.where(even > 0, even, 0) * (2.0 * math.pi / points)
    rate_odd = odd * (2.0 * math.pi / points)
    rates = np.broadcast_to(np.concatenate([rate_even, rate_odd]), (8, half))
    return table_even, table_odd, damp.reshape(groups, cells // groups, points), rates


def dot(a, b):
    return jnp.dot(a, b, preferred_element_type=jnp.float32)


def split(x):
    high = x.astype(jnp.bfloat16)
    return high, (x - high.astype(jnp.float32)).astype(jnp.bfloat16)


def dot_table(x, high_table, low_table):
    rows = x.shape[0]
    high, low = split(x)
    both = dot(jnp.concatenate([high, low], axis=0), high_table)
    return both[:rows] + (both[rows:] + dot(high, low_table))


def kernel(
    n_ax, n_xs,
    u_hbm, rate_hbm, swirl_hbm, dft_hbm, local_hbm, spikes_hbm, damp_hbm, rates_hbm, mix,
    out_ref,
    field, rate_ref, swirl_ref, dft, local, spikes, damp, rates,
    halo, inc, bound, solved, part, decay, lines, qe, qo, corr,
    load_sem, halo_send, halo_recv, inc_send, inc_recv, bound_send, bound_recv,
):
    planes, rows_all, points = field.shape
    half, quarter = points // 2, points // 4
    chunk = min(CHUNK, rows_all)
    chunks = rows_all // chunk
    ax, xs = lax.axis_index("ax"), lax.axis_index("xs")
    ahead, behind = lax.rem(ax + 1, n_ax), lax.rem(ax + n_ax - 1, n_ax)
    has_behind, has_ahead = ax > 0, ax < n_ax - 1

    loads = [
        pltpu.make_async_copy(source, target, load_sem.at[i])
        for i, (source, target) in enumerate(
            [
                (u_hbm, field),
                (local_hbm.at[xs], local),
                (spikes_hbm.at[xs], spikes),
                (dft_hbm, dft),
                (damp_hbm.at[xs], damp),
                (rates_hbm, rates),
                (swirl_hbm, swirl_ref),
                (rate_hbm, rate_ref),
            ]
        )
    ]
    for load in loads:
        load.start()

    barrier = pltpu.get_barrier_semaphore()

    @pl.when(has_behind)
    def _():
        pl.semaphore_signal(barrier, inc=1, device_id=(behind, xs), device_id_type=MESH)

    @pl.when(has_ahead)
    def _():
        pl.semaphore_signal(barrier, inc=1, device_id=(ahead, xs), device_id_type=MESH)

    for i in range(1, n_xs):
        pl.semaphore_signal(
            barrier, inc=1, device_id=(ax, lax.rem(xs + i, n_xs)), device_id_type=MESH
        )
    peers = n_xs - 1 + has_behind.astype(jnp.int32) + has_ahead.astype(jnp.int32)

    def rows_of(c):
        return pl.ds(pl.multiple_of(c * chunk, chunk), chunk)

    def halo_copy(s, side, c):
        start = planes - HALO if side == 0 else 0
        return pltpu.make_async_remote_copy(
            src_ref=solved.at[s, pl.ds(start, HALO), rows_of(c), :],
            dst_ref=halo.at[s, side, :, rows_of(c), :],
            send_sem=halo_send.at[s, side, c],
            recv_sem=halo_recv.at[s, side, c],
            device_id=(ahead if side == 0 else behind, xs),
            device_id_type=MESH,
        )

    def start_halo(s, c):
        @pl.when(has_ahead)
        def _():
            halo_copy(s, 0, c).start()

        @pl.when(has_behind)
        def _():
            halo_copy(s, 1, c).start()

    def relay_copy(s, c):
        source = field if s == 0 else out_ref
        return pltpu.make_async_remote_copy(
            src_ref=source.at[planes - 1, rows_of(c), :],
            dst_ref=inc.at[s, rows_of(c), :],
            send_sem=inc_send.at[s, c],
            recv_sem=inc_recv.at[s, c],
            device_id=(ahead, xs),
            device_id_type=MESH,
        )

    def bound_copy(s, i, owner):
        return pltpu.make_async_remote_copy(
            src_ref=bound.at[s, owner],
            dst_ref=bound.at[s, owner],
            send_sem=bound_send.at[s, i - 1],
            recv_sem=bound_recv.at[s, i - 1],
            device_id=(ax, lax.rem(xs + i, n_xs)),
            device_id_type=MESH,
        )

    def loop(body):
        lax.fori_loop(0, chunks, lambda c, carry: (body(c), carry)[1], 0)

    @pl.when(jnp.logical_not(has_behind))
    def _():
        halo[:, 0] = jnp.zeros_like(halo[:, 0])
        inc[...] = jnp.zeros_like(inc)

    @pl.when(jnp.logical_not(has_ahead))
    def _():
        halo[:, 1] = jnp.zeros_like(halo[:, 1])

    group = local.shape[1] // rows_all
    depth = group * rows_all
    for load in loads[:3]:
        load.wait()

    for s in range(SUBSTEPS):
        result = field if s == 0 else out_ref

        for first in range(0, planes, group):
            for column in range(0, points, 256):
                columns = slice(column, column + 256)
                x = field[first : first + group, :, columns].reshape(depth, 256)
                high, low = split(x)
                both = dot(local[...], high)
                x = both[:depth] + (both[depth:] + dot(local[:depth, :], low))
                for k in range(group):
                    here = x[k * rows_all : (k + 1) * rows_all]
                    solved[s, first + k, :, columns] = here
                    bound[s, xs, first + k : first + k + 1, columns] = here[:1]
                    place = planes + first + k
                    bound[s, xs, place : place + 1, columns] = here[rows_all - 1 :]
        if s == 0:
            pl.semaphore_wait(barrier, peers)
        for i in range(1, n_xs):
            bound_copy(s, i, xs).start()
        for i in range(1, n_xs):
            bound_copy(s, i, lax.rem(xs + n_xs - i, n_xs)).wait_recv()
        for side in range(2):
            total = jnp.zeros((planes, points), jnp.float32)
            for j in range(2 * n_xs):
                place = (j % 2) * planes
                total += mix[(xs * 2 + side) * 2 * n_xs + j] * bound[s, j // 2, place : place + planes, :]
            corr[side] = total

        def correct(c):
            rows = rows_of(c)
            spike = spikes[rows, :]
            left, right = spike[:, 0:1], spike[:, 1:2]
            for k in range(planes):
                solved[s, k, rows, :] += left * corr[0, k : k + 1, :] + right * corr[1, k : k + 1, :]
            start_halo(s, c)

        loop(correct)
        if s == 0:
            for load in loads[3:]:
                load.wait()

        def finish_rows(c):
            rows = rows_of(c)

            @pl.when(has_behind)
            def _():
                halo_copy(s, 0, c).wait_recv()

            @pl.when(has_ahead)
            def _():
                halo_copy(s, 1, c).wait_recv()

            def plane(k):
                if k < 0:
                    return halo[s, 0, k + HALO, rows, :]
                if k >= planes:
                    return halo[s, 1, k - planes, rows, :]
                return solved[s, k, rows, :]

            for k in range(planes):
                total = (1.0 + axial_weight * stencil_coeffs[0]) * plane(k)
                for d in range(1, HALO + 1):
                    total += axial_weight * stencil_coeffs[d] * (plane(k - d) + plane(k + d))
                lines[k * chunk : (k + 1) * chunk, :] = total
            low, high = lines[:, :half], lines[:, half:]
            even = dot_table(low + high, dft[0], dft[1])
            odd = dot_table(low - high, dft[2], dft[3])
            scale = damp[rows, :]
            rate_even, rate_odd = rates[0:1, :quarter], rates[0:1, quarter:]
            for k in range(planes):
                here = slice(k * chunk, (k + 1) * chunk)
                there = slice((planes + k) * chunk, (planes + k + 1) * chunk)
                value_even = even[here] * scale[:, :half]
                value_odd = odd[here] * scale[:, half:]
                qe[here, :] = value_even
                qo[here, :] = value_odd
                qe[there, :quarter] = rate_even * value_even[:, quarter:]
                qe[there, quarter:] = -rate_even * value_even[:, :quarter]
                qo[there, :quarter] = rate_odd * value_odd[:, quarter:]
                qo[there, quarter:] = -rate_odd * value_odd[:, :quarter]
            qe[...] = dot_table(qe[...], dft[4], dft[5])
            qo[...] = dot_table(qo[...], dft[6], dft[7])
            for side in range(2):
                columns = slice(side * half, (side + 1) * half)
                value = jnp.zeros((chunk, half), jnp.float32)
                product = jnp.ones((chunk, half), jnp.float32)
                for k in range(planes):
                    here = slice(k * chunk, (k + 1) * chunk)
                    there = slice((planes + k) * chunk, (planes + k + 1) * chunk)
                    if side == 0:
                        smooth, slope = qe[here, :] + qo[here, :], qe[there, :] + qo[there, :]
                    else:
                        smooth, slope = qe[here, :] - qo[here, :], qe[there, :] - qo[there, :]
                    courant = CZ * rate_ref[k, rows, columns]
                    inverse = 1.0 / (1.0 + courant)
                    factor = courant * inverse
                    value = inverse * (smooth - swirl_ref[k, rows, columns] * slope) + factor * value
                    product = factor * product
                    part[k, :, columns] = value
                    decay[k, :, columns] = product

            @pl.when(has_behind)
            def _():
                relay_copy(s, c).wait_recv()

            last = planes - 1
            entering = inc[s, rows, :]
            result[last, rows, :] = part[last] + decay[last] * entering

            @pl.when(has_ahead)
            def _():
                relay_copy(s, c).start()

            for k in range(last):
                result[k, rows, :] = part[k] + decay[k] * entering

        loop(finish_rows)

    for s in range(SUBSTEPS):

        def finish(c):
            @pl.when(has_ahead)
            def _():
                halo_copy(s, 0, c).wait_send()
                relay_copy(s, c).wait_send()

            @pl.when(has_behind)
            def _():
                halo_copy(s, 1, c).wait_send()

        loop(finish)
        for i in range(1, n_xs):
            bound_copy(s, i, xs).wait_send()


def solution(mesh):
    n_ax, n_xs = mesh.shape["ax"], mesh.shape["xs"]

    def body(scalar, axial_rate, swirl_rate):
        planes, rows, points = scalar.shape
        cells = rows * n_xs
        chunk = min(CHUNK, rows)
        chunks = rows // chunk
        half = points // 2
        local, spikes, mix = radial_tables(cells, n_xs)
        even, odd, damp, rates = azimuth_tables(points, cells, n_xs)
        pairs = [split_table(x) for x in (even, odd, even.T, odd.T)]
        dft = np.stack([x for pair in pairs for x in pair])
        group = min(planes, 256 // rows)
        blocks = np.stack([np.kron(np.eye(group), x) for x in local])
        blocks = np.concatenate(split_table(blocks), axis=1)
        spikes = np.pad(spikes, ((0, 0), (0, 0), (0, 126))).astype(np.float32)
        tables = [dft, blocks, spikes, damp.astype(np.float32), rates.astype(np.float32)]
        f32 = jnp.float32
        block = pltpu.VMEM((planes, rows, points), f32)
        part = pltpu.VMEM((planes, chunk, points), f32)
        pair = pltpu.VMEM((2 * planes * chunk, half), f32)
        dma = pltpu.SemaphoreType.DMA
        return pl.pallas_call(
            functools.partial(kernel, n_ax, n_xs),
            out_shape=jax.ShapeDtypeStruct(scalar.shape, f32),
            in_specs=[pl.BlockSpec(memory_space=pl.ANY)] * (3 + len(tables))
            + [pl.BlockSpec(memory_space=pltpu.SMEM)],
            out_specs=pl.BlockSpec(memory_space=pltpu.VMEM),
            scratch_shapes=[
                block, block, block,
                pltpu.VMEM(dft.shape, jnp.bfloat16),
                pltpu.VMEM(blocks.shape[1:], jnp.bfloat16),
                pltpu.VMEM(spikes.shape[1:], f32),
                pltpu.VMEM(damp.shape[1:], f32),
                pltpu.VMEM(rates.shape, f32),
                pltpu.VMEM((SUBSTEPS, 2, HALO, rows, points), f32),
                pltpu.VMEM((SUBSTEPS, rows, points), f32),
                pltpu.VMEM((SUBSTEPS, n_xs, 2 * planes, points), f32),
                pltpu.VMEM((SUBSTEPS, planes, rows, points), f32),
                part, part,
                pltpu.VMEM((planes * chunk, points), f32),
                pair, pair,
                pltpu.VMEM((2, planes, points), f32),
                dma((8,)),
                dma((SUBSTEPS, 2, chunks)), dma((SUBSTEPS, 2, chunks)),
                dma((SUBSTEPS, chunks)), dma((SUBSTEPS, chunks)),
                dma((SUBSTEPS, n_xs - 1)), dma((SUBSTEPS, n_xs - 1)),
            ],
            compiler_params=pltpu.CompilerParams(
                collective_id=0, has_side_effects=True, vmem_limit_bytes=62 * 2**20
            ),
        )(
            scalar, axial_rate, swirl_rate,
            *[jnp.asarray(t) for t in tables],
            jnp.asarray(mix.reshape(-1).astype(np.float32)),
        )

    return jax.shard_map(
        body,
        mesh=mesh,
        in_specs=(P("ax", "xs", None), P("ax", "xs", None), P("ax", "xs", None)),
        out_specs=P("ax", "xs", None),
        check_vma=False,
    )
```

```python
import functools
import math

import jax
import jax.numpy as jnp
import ml_dtypes
import numpy as np
from jax import lax
from jax.experimental import pallas as pl
from jax.experimental.pallas import tpu as pltpu
from jax.sharding import PartitionSpec as P

CZ = 8
SUBSTEPS = 2
HALO = 4
CHUNK = 16
MESH = pl.DeviceIdType.MESH

axial_weight = 0.2
azimuth_damp = 0.5
diffusion_number = 1.0
stencil_coeffs = (
    -205.0 / 72.0,
    1.6,
    -0.2,
    8.0 / 315.0,
    -1.0 / 560.0,
)


def split_table(table):
    high = table.astype(np.float32).astype(ml_dtypes.bfloat16)
    low = (table - high.astype(np.float64)).astype(np.float32).astype(ml_dtypes.bfloat16)
    return high, low


def radial_tables(cells, groups):
    rows = cells // groups
    index = np.arange(cells, dtype=np.float64)
    radius = index + 0.5
    upper = np.where(index < cells - 1, index + 1.0, 0.0)
    sub = -diffusion_number * index / radius
    sup = -diffusion_number * upper / radius
    full = np.diag(1.0 - sub - sup) + np.diag(sub[1:], -1) + np.diag(sup[:-1], 1)
    local = np.zeros((groups, rows, rows))
    spikes = np.zeros((groups, rows, 2))
    coupling = np.zeros((2 * groups, 2 * groups))
    for d in range(groups):
        first, last = d * rows, (d + 1) * rows - 1
        local[d] = np.linalg.inv(full[first : last + 1, first : last + 1])
        if d > 0:
            spikes[d, :, 0] = -local[d][:, 0] * sub[first]
            coupling[2 * d, 2 * d - 1] = spikes[d, 0, 0]
            coupling[2 * d + 1, 2 * d - 1] = spikes[d, -1, 0]
        if d < groups - 1:
            spikes[d, :, 1] = -local[d][:, -1] * sup[last]
            coupling[2 * d, 2 * d + 2] = spikes[d, 0, 1]
            coupling[2 * d + 1, 2 * d + 2] = spikes[d, -1, 1]
    reduced = np.linalg.inv(np.eye(2 * groups) - coupling)
    mix = np.zeros((groups, 2, 2 * groups))
    for d in range(groups):
        if d > 0:
            mix[d, 0] = reduced[2 * d - 1]
        if d < groups - 1:
            mix[d, 1] = reduced[2 * d + 2]
    return local, spikes, mix


def azimuth_tables(points, cells, groups):
    half, quarter = points // 2, points // 4
    grid = np.arange(half)
    even, odd = 2 * np.arange(quarter), 2 * np.arange(quarter) + 1

    def angle(m):
        return (grid[:, None] * m[None, :] % points) * (2.0 * math.pi / points)

    sine_even = np.sin(angle(even))
    sine_even[:, 0] = np.cos(math.pi * grid)
    table_even = np.concatenate([np.cos(angle(even)), sine_even], axis=1)
    table_odd = np.concatenate([np.cos(angle(odd)), np.sin(angle(odd))], axis=1)
    sine_m = even.copy()
    sine_m[0] = half
    wave = np.concatenate([even, sine_m, odd, odd]).astype(np.float64)
    weight = np.where((wave == 0) | (wave == half), 1.0, 2.0) / points
    radius = np.arange(cells) + 0.5
    damp = weight / (1.0 + azimuth_damp * wave[None, :] ** 2 / radius[:, None] ** 2)
    rate_even = np.where(even > 0, even, 0) * (2.0 * math.pi / points)
    rate_odd = odd * (2.0 * math.pi / points)
    rates = np.broadcast_to(np.concatenate([rate_even, rate_odd]), (8, half))
    return table_even, table_odd, damp.reshape(groups, cells // groups, points), rates


def dot(a, b):
    return jnp.dot(a, b, preferred_element_type=jnp.float32)


def split(x):
    high = x.astype(jnp.bfloat16)
    return high, (x - high.astype(jnp.float32)).astype(jnp.bfloat16)


def dot_table(x, high_table, low_table):
    rows = x.shape[0]
    high, low = split(x)
    both = dot(jnp.concatenate([high, low], axis=0), high_table)
    return both[:rows] + (both[rows:] + dot(high, low_table))


def kernel(
    n_ax, n_xs,
    u_hbm, rate_hbm, swirl_hbm, dft_hbm, local_hbm, spikes_hbm, damp_hbm, rates_hbm, mix,
    out_ref,
    field, rate_ref, swirl_ref, dft, local, spikes, damp, rates,
    halo, inc, bound, solved, part, decay, lines, qe, qo, corr,
    load_sem, halo_send, halo_recv, inc_send, inc_recv, bound_send, bound_recv,
):
    planes, rows_all, points = field.shape
    half, quarter = points // 2, points // 4
    chunk = min(CHUNK, rows_all)
    chunks = rows_all // chunk
    ax, xs = lax.axis_index("ax"), lax.axis_index("xs")
    ahead, behind = lax.rem(ax + 1, n_ax), lax.rem(ax + n_ax - 1, n_ax)
    has_behind, has_ahead = ax > 0, ax < n_ax - 1

    loads = [
        pltpu.make_async_copy(source, target, load_sem.at[i])
        for i, (source, target) in enumerate(
            [
                (u_hbm, field),
                (local_hbm.at[xs], local),
                (spikes_hbm.at[xs], spikes),
                (dft_hbm, dft),
                (damp_hbm.at[xs], damp),
                (rates_hbm, rates),
                (swirl_hbm, swirl_ref),
                (rate_hbm, rate_ref),
            ]
        )
    ]
    for load in loads:
        load.start()

    barrier = pltpu.get_barrier_semaphore()

    @pl.when(has_behind)
    def _():
        pl.semaphore_signal(barrier, inc=1, device_id=(behind, xs), device_id_type=MESH)

    @pl.when(has_ahead)
    def _():
        pl.semaphore_signal(barrier, inc=1, device_id=(ahead, xs), device_id_type=MESH)

    for i in range(1, n_xs):
        pl.semaphore_signal(
            barrier, inc=1, device_id=(ax, lax.rem(xs + i, n_xs)), device_id_type=MESH
        )
    peers = n_xs - 1 + has_behind.astype(jnp.int32) + has_ahead.astype(jnp.int32)

    def rows_of(c):
        return pl.ds(pl.multiple_of(c * chunk, chunk), chunk)

    def halo_copy(s, side, c):
        start = planes - HALO if side == 0 else 0
        return pltpu.make_async_remote_copy(
            src_ref=solved.at[s, pl.ds(start, HALO), rows_of(c), :],
            dst_ref=halo.at[s, side, :, rows_of(c), :],
            send_sem=halo_send.at[s, side, c],
            recv_sem=halo_recv.at[s, side, c],
            device_id=(ahead if side == 0 else behind, xs),
            device_id_type=MESH,
        )

    def start_halo(s, c):
        @pl.when(has_ahead)
        def _():
            halo_copy(s, 0, c).start()

        @pl.when(has_behind)
        def _():
            halo_copy(s, 1, c).start()

    def relay_copy(s, c):
        source = field if s == 0 else out_ref
        return pltpu.make_async_remote_copy(
            src_ref=source.at[planes - 1, rows_of(c), :],
            dst_ref=inc.at[s, rows_of(c), :],
            send_sem=inc_send.at[s, c],
            recv_sem=inc_recv.at[s, c],
            device_id=(ahead, xs),
            device_id_type=MESH,
        )

    def bound_copy(s, i, owner):
        return pltpu.make_async_remote_copy(
            src_ref=bound.at[s, owner],
            dst_ref=bound.at[s, owner],
            send_sem=bound_send.at[s, i - 1],
            recv_sem=bound_recv.at[s, i - 1],
            device_id=(ax, lax.rem(xs + i, n_xs)),
            device_id_type=MESH,
        )

    def loop(body):
        lax.fori_loop(0, chunks, lambda c, carry: (body(c), carry)[1], 0)

    @pl.when(jnp.logical_not(has_behind))
    def _():
        halo[:, 0] = jnp.zeros_like(halo[:, 0])
        inc[...] = jnp.zeros_like(inc)

    @pl.when(jnp.logical_not(has_ahead))
    def _():
        halo[:, 1] = jnp.zeros_like(halo[:, 1])

    group = local.shape[1] // rows_all
    depth = group * rows_all
    for load in loads[:3]:
        load.wait()

    for s in range(SUBSTEPS):
        result = field if s == 0 else out_ref

        for first in range(0, planes, group):
            for column in range(0, points, 256):
                columns = slice(column, column + 256)
                x = field[first : first + group, :, columns].reshape(depth, 256)
                high, low = split(x)
                both = dot(local[...], high)
                x = both[:depth] + (both[depth:] + dot(local[:depth, :], low))
                for k in range(group):
                    here = x[k * rows_all : (k + 1) * rows_all]
                    solved[s, first + k, :, columns] = here
                    bound[s, xs, first + k : first + k + 1, columns] = here[:1]
                    place = planes + first + k
                    bound[s, xs, place : place + 1, columns] = here[rows_all - 1 :]
        if s == 0:
            pl.semaphore_wait(barrier, peers)
        for i in range(1, n_xs):
            bound_copy(s, i, xs).start()
        for i in range(1, n_xs):
            bound_copy(s, i, lax.rem(xs + n_xs - i, n_xs)).wait_recv()
        for side in range(2):
            total = jnp.zeros((planes, points), jnp.float32)
            for j in range(2 * n_xs):
                place = (j % 2) * planes
                total += mix[(xs * 2 + side) * 2 * n_xs + j] * bound[s, j // 2, place : place + planes, :]
            corr[side] = total

        def correct(c):
            rows = rows_of(c)
            spike = spikes[rows, :]
            left, right = spike[:, 0:1], spike[:, 1:2]
            for k in range(planes):
                solved[s, k, rows, :] += left * corr[0, k : k + 1, :] + right * corr[1, k : k + 1, :]
            start_halo(s, c)

        loop(correct)
        if s == 0:
            for load in loads[3:]:
                load.wait()

        def finish_rows(c):
            rows = rows_of(c)

            @pl.when(has_behind)
            def _():
                halo_copy(s, 0, c).wait_recv()

            @pl.when(has_ahead)
            def _():
                halo_copy(s, 1, c).wait_recv()

            def plane(k):
                if k < 0:
                    return halo[s, 0, k + HALO, rows, :]
                if k >= planes:
                    return halo[s, 1, k - planes, rows, :]
                return solved[s, k, rows, :]

            for k in range(planes):
                total = (1.0 + axial_weight * stencil_coeffs[0]) * plane(k)
                for d in range(1, HALO + 1):
                    total += axial_weight * stencil_coeffs[d] * (plane(k - d) + plane(k + d))
                lines[k * chunk : (k + 1) * chunk, :] = total
            low, high = lines[:, :half], lines[:, half:]
            even = dot_table(low + high, dft[0], dft[1])
            odd = dot_table(low - high, dft[2], dft[3])
            scale = damp[rows, :]
            rate_even, rate_odd = rates[0:1, :quarter], rates[0:1, quarter:]
            for k in range(planes):
                here = slice(k * chunk, (k + 1) * chunk)
                there = slice((planes + k) * chunk, (planes + k + 1) * chunk)
                value_even = even[here] * scale[:, :half]
                value_odd = odd[here] * scale[:, half:]
                qe[here, :] = value_even
                qo[here, :] = value_odd
                qe[there, :quarter] = rate_even * value_even[:, quarter:]
                qe[there, quarter:] = -rate_even * value_even[:, :quarter]
                qo[there, :quarter] = rate_odd * value_odd[:, quarter:]
                qo[there, quarter:] = -rate_odd * value_odd[:, :quarter]
            qe[...] = dot_table(qe[...], dft[4], dft[5])
            qo[...] = dot_table(qo[...], dft[6], dft[7])
            for side in range(2):
                columns = slice(side * half, (side + 1) * half)
                value = jnp.zeros((chunk, half), jnp.float32)
                product = jnp.ones((chunk, half), jnp.float32)
                for k in range(planes):
                    here = slice(k * chunk, (k + 1) * chunk)
                    there = slice((planes + k) * chunk, (planes + k + 1) * chunk)
                    if side == 0:
                        smooth, slope = qe[here, :] + qo[here, :], qe[there, :] + qo[there, :]
                    else:
                        smooth, slope = qe[here, :] - qo[here, :], qe[there, :] - qo[there, :]
                    courant = CZ * rate_ref[k, rows, columns]
                    inverse = 1.0 / (1.0 + courant)
                    factor = courant * inverse
                    value = inverse * (smooth - swirl_ref[k, rows, columns] * slope) + factor * value
                    product = factor * product
                    part[k, rows, columns] = value
                    decay[k, rows, columns] = product

        loop(finish_rows)

        def relay(c):
            rows = rows_of(c)

            @pl.when(has_behind)
            def _():
                relay_copy(s, c).wait_recv()

            last = planes - 1
            entering = inc[s, rows, :]
            result[last, rows, :] = part[last, rows, :] + decay[last, rows, :] * entering

            @pl.when(has_ahead)
            def _():
                relay_copy(s, c).start()

            for k in range(last):
                result[k, rows, :] = part[k, rows, :] + decay[k, rows, :] * entering

        loop(relay)

    for s in range(SUBSTEPS):

        def finish(c):
            @pl.when(has_ahead)
            def _():
                halo_copy(s, 0, c).wait_send()
                relay_copy(s, c).wait_send()

            @pl.when(has_behind)
            def _():
                halo_copy(s, 1, c).wait_send()

        loop(finish)
        for i in range(1, n_xs):
            bound_copy(s, i, xs).wait_send()


def solution(mesh):
    n_ax, n_xs = mesh.shape["ax"], mesh.shape["xs"]

    def body(scalar, axial_rate, swirl_rate):
        planes, rows, points = scalar.shape
        cells = rows * n_xs
        chunk = min(CHUNK, rows)
        chunks = rows // chunk
        half = points // 2
        local, spikes, mix = radial_tables(cells, n_xs)
        even, odd, damp, rates = azimuth_tables(points, cells, n_xs)
        pairs = [split_table(x) for x in (even, odd, even.T, odd.T)]
        dft = np.stack([x for pair in pairs for x in pair])
        group = min(planes, 256 // rows)
        blocks = np.stack([np.kron(np.eye(group), x) for x in local])
        blocks = np.concatenate(split_table(blocks), axis=1)
        spikes = np.pad(spikes, ((0, 0), (0, 0), (0, 126))).astype(np.float32)
        tables = [dft, blocks, spikes, damp.astype(np.float32), rates.astype(np.float32)]
        f32 = jnp.float32
        block = pltpu.VMEM((planes, rows, points), f32)
        pair = pltpu.VMEM((2 * planes * chunk, half), f32)
        dma = pltpu.SemaphoreType.DMA
        return pl.pallas_call(
            functools.partial(kernel, n_ax, n_xs),
            out_shape=jax.ShapeDtypeStruct(scalar.shape, f32),
            in_specs=[pl.BlockSpec(memory_space=pl.ANY)] * (3 + len(tables))
            + [pl.BlockSpec(memory_space=pltpu.SMEM)],
            out_specs=pl.BlockSpec(memory_space=pltpu.VMEM),
            scratch_shapes=[
                block, block, block,
                pltpu.VMEM(dft.shape, jnp.bfloat16),
                pltpu.VMEM(blocks.shape[1:], jnp.bfloat16),
                pltpu.VMEM(spikes.shape[1:], f32),
                pltpu.VMEM(damp.shape[1:], f32),
                pltpu.VMEM(rates.shape, f32),
                pltpu.VMEM((SUBSTEPS, 2, HALO, rows, points), f32),
                pltpu.VMEM((SUBSTEPS, rows, points), f32),
                pltpu.VMEM((SUBSTEPS, n_xs, 2 * planes, points), f32),
                pltpu.VMEM((SUBSTEPS, planes, rows, points), f32),
                block, block,
                pltpu.VMEM((planes * chunk, points), f32),
                pair, pair,
                pltpu.VMEM((2, planes, points), f32),
                dma((8,)),
                dma((SUBSTEPS, 2, chunks)), dma((SUBSTEPS, 2, chunks)),
                dma((SUBSTEPS, chunks)), dma((SUBSTEPS, chunks)),
                dma((SUBSTEPS, n_xs - 1)), dma((SUBSTEPS, n_xs - 1)),
            ],
            compiler_params=pltpu.CompilerParams(
                collective_id=0, has_side_effects=True, vmem_limit_bytes=62 * 2**20
            ),
        )(
            scalar, axial_rate, swirl_rate,
            *[jnp.asarray(t) for t in tables],
            jnp.asarray(mix.reshape(-1).astype(np.float32)),
        )

    return jax.shard_map(
        body,
        mesh=mesh,
        in_specs=(P("ax", "xs", None), P("ax", "xs", None), P("ax", "xs", None)),
        out_specs=P("ax", "xs", None),
        check_vma=False,
    )
```

```python
import functools
import math

import jax
import jax.numpy as jnp
import ml_dtypes
import numpy as np
from jax import lax
from jax.experimental import pallas as pl
from jax.experimental.pallas import tpu as pltpu
from jax.sharding import PartitionSpec as P

CZ = 8
SUBSTEPS = 2
HALO = 4
CHUNK = 16
MESH = pl.DeviceIdType.MESH

axial_weight = 0.2
azimuth_damp = 0.5
diffusion_number = 1.0
stencil_coeffs = (
    -205.0 / 72.0,
    1.6,
    -0.2,
    8.0 / 315.0,
    -1.0 / 560.0,
)


def split_table(table):
    high = table.astype(np.float32).astype(ml_dtypes.bfloat16)
    low = (table - high.astype(np.float64)).astype(np.float32).astype(ml_dtypes.bfloat16)
    return high, low


def radial_tables(cells, groups):
    rows = cells // groups
    index = np.arange(cells, dtype=np.float64)
    radius = index + 0.5
    upper = np.where(index < cells - 1, index + 1.0, 0.0)
    sub = -diffusion_number * index / radius
    sup = -diffusion_number * upper / radius
    full = np.diag(1.0 - sub - sup) + np.diag(sub[1:], -1) + np.diag(sup[:-1], 1)
    local = np.zeros((groups, rows, rows))
    spikes = np.zeros((groups, rows, 2))
    coupling = np.zeros((2 * groups, 2 * groups))
    for d in range(groups):
        first, last = d * rows, (d + 1) * rows - 1
        local[d] = np.linalg.inv(full[first : last + 1, first : last + 1])
        if d > 0:
            spikes[d, :, 0] = -local[d][:, 0] * sub[first]
            coupling[2 * d, 2 * d - 1] = spikes[d, 0, 0]
            coupling[2 * d + 1, 2 * d - 1] = spikes[d, -1, 0]
        if d < groups - 1:
            spikes[d, :, 1] = -local[d][:, -1] * sup[last]
            coupling[2 * d, 2 * d + 2] = spikes[d, 0, 1]
            coupling[2 * d + 1, 2 * d + 2] = spikes[d, -1, 1]
    reduced = np.linalg.inv(np.eye(2 * groups) - coupling)
    mix = np.zeros((groups, 2, 2 * groups))
    for d in range(groups):
        if d > 0:
            mix[d, 0] = reduced[2 * d - 1]
        if d < groups - 1:
            mix[d, 1] = reduced[2 * d + 2]
    return local, spikes, mix


def chunk_tables(cells, groups, chunk):
    rows = cells // groups
    chunks = rows // chunk
    edges = 2 * chunks
    local, spikes, _ = radial_tables(cells, groups * chunks)
    _, outer, mix = radial_tables(cells, groups)
    weights = []
    for d in range(groups):
        coupling = np.zeros((edges, edges))
        for c in range(chunks):
            spike = spikes[d * chunks + c]
            for side, row in ((0, 0), (1, -1)):
                if c > 0:
                    coupling[2 * c + side, 2 * c - 1] = spike[row, 0]
                if c < chunks - 1:
                    coupling[2 * c + side, 2 * c + 2] = spike[row, 1]
        inner = np.linalg.inv(np.eye(edges) - coupling)
        near = np.zeros((edges, edges + 2))
        for c in range(chunks):
            if c > 0:
                near[2 * c, :edges] = inner[2 * c - 1]
                near[2 * c, edges:] = outer[d, c * chunk - 1]
            else:
                near[0, edges] = 1.0
            if c < chunks - 1:
                near[2 * c + 1, :edges] = inner[2 * c + 2]
                near[2 * c + 1, edges:] = outer[d, (c + 1) * chunk]
            else:
                near[2 * c + 1, edges + 1] = 1.0
        ends = inner[[0, -1]]
        weights.append(np.concatenate([ends.reshape(-1), mix[d].reshape(-1), near.reshape(-1)]))
    return local, spikes.reshape(groups, rows, 2), np.stack(weights)


def azimuth_tables(points, cells, groups):
    half, quarter = points // 2, points // 4
    grid = np.arange(half)
    even, odd = 2 * np.arange(quarter), 2 * np.arange(quarter) + 1

    def angle(m):
        return (grid[:, None] * m[None, :] % points) * (2.0 * math.pi / points)

    sine_even = np.sin(angle(even))
    sine_even[:, 0] = np.cos(math.pi * grid)
    table_even = np.concatenate([np.cos(angle(even)), sine_even], axis=1)
    table_odd = np.concatenate([np.cos(angle(odd)), np.sin(angle(odd))], axis=1)
    sine_m = even.copy()
    sine_m[0] = half
    wave = np.concatenate([even, sine_m, odd, odd]).astype(np.float64)
    weight = np.where((wave == 0) | (wave == half), 1.0, 2.0) / points
    radius = np.arange(cells) + 0.5
    damp = weight / (1.0 + azimuth_damp * wave[None, :] ** 2 / radius[:, None] ** 2)
    rate_even = np.where(even > 0, even, 0) * (2.0 * math.pi / points)
    rate_odd = odd * (2.0 * math.pi / points)
    rates = np.broadcast_to(np.concatenate([rate_even, rate_odd]), (8, half))
    return table_even, table_odd, damp.reshape(groups, cells // groups, points), rates


def dot(a, b):
    return jnp.dot(a, b, preferred_element_type=jnp.float32)


def split(x):
    high = x.astype(jnp.bfloat16)
    return high, (x - high.astype(jnp.float32)).astype(jnp.bfloat16)


def dot_table(x, high_table, low_table):
    rows = x.shape[0]
    high, low = split(x)
    both = dot(jnp.concatenate([high, low], axis=0), high_table)
    return both[:rows] + (both[rows:] + dot(high, low_table))


def kernel(
    n_ax, n_xs,
    u_hbm, rate_hbm, swirl_hbm, dft_hbm, local_hbm, spikes_hbm, damp_hbm, rates_hbm, mix,
    out_ref,
    field, rate_ref, swirl_ref, dft, local, spikes, damp, rates,
    halo, inc, bound, solved, part, decay, lines, qe, qo, corr, edge, pack, side_halo, extended,
    load_sem, halo_send, halo_recv, side_send, side_recv, inc_send, inc_recv, bound_send, bound_recv,
):
    planes, rows_all, points = field.shape
    half, quarter = points // 2, points // 4
    chunk = min(CHUNK, rows_all)
    chunks = rows_all // chunk
    ax, xs = lax.axis_index("ax"), lax.axis_index("xs")
    ahead, behind = lax.rem(ax + 1, n_ax), lax.rem(ax + n_ax - 1, n_ax)
    has_behind, has_ahead = ax > 0, ax < n_ax - 1

    loads = [
        pltpu.make_async_copy(source, target, load_sem.at[i])
        for i, (source, target) in enumerate(
            [
                (u_hbm, field),
                (local_hbm.at[xs], local),
                (spikes_hbm.at[xs], spikes),
                (dft_hbm, dft),
                (damp_hbm.at[xs], damp),
                (rates_hbm, rates),
                (swirl_hbm, swirl_ref),
                (rate_hbm, rate_ref),
            ]
        )
    ]
    for load in loads:
        load.start()

    barrier = pltpu.get_barrier_semaphore()

    @pl.when(has_behind)
    def _():
        pl.semaphore_signal(barrier, inc=1, device_id=(behind, xs), device_id_type=MESH)

    @pl.when(has_ahead)
    def _():
        pl.semaphore_signal(barrier, inc=1, device_id=(ahead, xs), device_id_type=MESH)

    for i in range(1, n_xs):
        pl.semaphore_signal(
            barrier, inc=1, device_id=(ax, lax.rem(xs + i, n_xs)), device_id_type=MESH
        )
    peers = n_xs - 1 + has_behind.astype(jnp.int32) + has_ahead.astype(jnp.int32)

    def rows_of(c):
        return pl.ds(pl.multiple_of(c * chunk, chunk), chunk)

    def halo_copy(s, side, c):
        start = planes - HALO if side == 0 else 0
        return pltpu.make_async_remote_copy(
            src_ref=solved.at[s, pl.ds(start, HALO), rows_of(c), :],
            dst_ref=halo.at[s, side, :, rows_of(c), :],
            send_sem=halo_send.at[s, side, c],
            recv_sem=halo_recv.at[s, side, c],
            device_id=(ahead if side == 0 else behind, xs),
            device_id_type=MESH,
        )

    def start_halo(s, c):
        @pl.when(has_ahead)
        def _():
            halo_copy(s, 0, c).start()

        @pl.when(has_behind)
        def _():
            halo_copy(s, 1, c).start()

    def side_copy(s, side):
        return pltpu.make_async_remote_copy(
            src_ref=pack.at[s, side],
            dst_ref=side_halo.at[s, side],
            send_sem=side_send.at[s, side],
            recv_sem=side_recv.at[s, side],
            device_id=(ahead if side == 0 else behind, xs),
            device_id_type=MESH,
        )

    def relay_copy(s, c):
        source = field if s == 0 else out_ref
        return pltpu.make_async_remote_copy(
            src_ref=source.at[planes - 1, rows_of(c), :],
            dst_ref=inc.at[s, rows_of(c), :],
            send_sem=inc_send.at[s, c],
            recv_sem=inc_recv.at[s, c],
            device_id=(ahead, xs),
            device_id_type=MESH,
        )

    def bound_copy(s, i, owner):
        return pltpu.make_async_remote_copy(
            src_ref=bound.at[s, owner],
            dst_ref=bound.at[s, owner],
            send_sem=bound_send.at[s, i - 1],
            recv_sem=bound_recv.at[s, i - 1],
            device_id=(ax, lax.rem(xs + i, n_xs)),
            device_id_type=MESH,
        )

    def loop(body):
        lax.fori_loop(0, chunks, lambda c, carry: (body(c), carry)[1], 0)

    @pl.when(jnp.logical_not(has_behind))
    def _():
        halo[:, 0] = jnp.zeros_like(halo[:, 0])
        side_halo[:, 0] = jnp.zeros_like(side_halo[:, 0])
        inc[...] = jnp.zeros_like(inc)

    @pl.when(jnp.logical_not(has_ahead))
    def _():
        halo[:, 1] = jnp.zeros_like(halo[:, 1])
        side_halo[:, 1] = jnp.zeros_like(side_halo[:, 1])

    edges = 2 * chunks
    near_at = 2 * edges + 4 * n_xs
    stride = near_at + edges * (edges + 2)

    def solve_chunk(s, c):
        rows = rows_of(c)
        depth = planes * chunk
        for column in range(0, points, half):
            columns = slice(column, column + half)
            high, low = split(field[:, rows, columns].reshape(depth, half))
            both = dot(local[c], high)
            x = both[:depth] + (both[depth:] + dot(local[c, :depth, :], low))
            for k in range(planes):
                here = x[k * chunk : (k + 1) * chunk]
                solved[s, k, rows, columns] = here
                edge[c, 0, k : k + 1, columns] = here[:1]
                edge[c, 1, k : k + 1, columns] = here[chunk - 1 :]

    def mixed(start, terms):
        total = jnp.zeros((planes, points), jnp.float32)
        for j, term in enumerate(terms):
            total += mix[xs * stride + start + j] * term()
        return total

    def join_chunks(s):
        inner = [lambda j=j: edge[j // 2, j % 2] for j in range(edges)]
        outer = [lambda j=j: bound[s, j // 2, (j % 2) * planes : (j % 2 + 1) * planes] for j in range(2 * n_xs)]
        for side in range(2):
            bound[s, xs, side * planes : (side + 1) * planes, :] = mixed(side * edges, inner)
        if s == 0:
            pl.semaphore_wait(barrier, peers)
            lax.fori_loop(0, early[0], lambda c, carry: (start_halo(0, c), carry)[1], 0)
        for i in range(1, n_xs):
            bound_copy(s, i, xs).start()
        for i in range(1, n_xs):
            bound_copy(s, i, lax.rem(xs + n_xs - i, n_xs)).wait_recv()
        for side in range(2):
            corr[edges + side] = mixed(2 * edges + side * 2 * n_xs, outer)
        inner += [lambda: corr[edges], lambda: corr[edges + 1]]
        for c in range(chunks):
            values = []
            for side in range(2):
                j = 2 * c + side
                value = mixed(near_at + j * (edges + 2), inner)
                corr[j] = value
                values.append(value)
            pack[s, 0, c] = jnp.concatenate([x[planes - HALO :] for x in values], axis=0)
            pack[s, 1, c] = jnp.concatenate([x[:HALO] for x in values], axis=0)

        @pl.when(has_ahead)
        def _():
            side_copy(s, 0).start()

        @pl.when(has_behind)
        def _():
            side_copy(s, 1).start()

        lax.fori_loop(early[s], chunks, lambda c, carry: (start_halo(s, c), carry)[1], 0)

    early = (min(1, chunks - 1), chunks - 1)
    for load in loads[:3]:
        load.wait()
    loop(lambda c: solve_chunk(0, c))

    for s in range(SUBSTEPS):
        result = field if s == 0 else out_ref
        join_chunks(s)
        if s == 0:
            for load in loads[3:]:
                load.wait()

        @pl.when(has_behind)
        def _():
            side_copy(s, 0).wait_recv()

        @pl.when(has_ahead)
        def _():
            side_copy(s, 1).wait_recv()

        def finish_rows(c):
            rows = rows_of(c)

            @pl.when(has_behind)
            def _():
                halo_copy(s, 0, c).wait_recv()

            @pl.when(has_ahead)
            def _():
                halo_copy(s, 1, c).wait_recv()

            def plane(k):
                if k < 0:
                    return halo[s, 0, k + HALO, rows, :]
                if k >= planes:
                    return halo[s, 1, k - planes, rows, :]
                return solved[s, k, rows, :]

            centre = 1.0 + axial_weight * stencil_coeffs[0]
            spike = spikes[rows, :]
            for side in range(2):
                extended[side, :HALO] = side_halo[s, 0, c, side * HALO : (side + 1) * HALO]
                extended[side, HALO : HALO + planes] = corr[2 * c + side]
                extended[side, HALO + planes :] = side_halo[s, 1, c, side * HALO : (side + 1) * HALO]
            sides = []
            for side in range(2):
                total = centre * extended[side, HALO : HALO + planes]
                for d in range(1, HALO + 1):
                    total += axial_weight * stencil_coeffs[d] * (
                        extended[side, HALO - d : HALO - d + planes]
                        + extended[side, HALO + d : HALO + d + planes]
                    )
                sides.append(total)
            for k in range(planes):
                total = centre * plane(k)
                for d in range(1, HALO + 1):
                    total += axial_weight * stencil_coeffs[d] * (plane(k - d) + plane(k + d))
                total += spike[:, 0:1] * sides[0][k : k + 1] + spike[:, 1:2] * sides[1][k : k + 1]
                lines[k * chunk : (k + 1) * chunk, :] = total
            low, high = lines[:, :half], lines[:, half:]
            even = dot_table(low + high, dft[0], dft[1])
            odd = dot_table(low - high, dft[2], dft[3])
            scale = damp[rows, :]
            rate_even, rate_odd = rates[0:1, :quarter], rates[0:1, quarter:]
            for k in range(planes):
                here = slice(k * chunk, (k + 1) * chunk)
                there = slice((planes + k) * chunk, (planes + k + 1) * chunk)
                value_even = even[here] * scale[:, :half]
                value_odd = odd[here] * scale[:, half:]
                qe[here, :] = value_even
                qo[here, :] = value_odd
                qe[there, :quarter] = rate_even * value_even[:, quarter:]
                qe[there, quarter:] = -rate_even * value_even[:, :quarter]
                qo[there, :quarter] = rate_odd * value_odd[:, quarter:]
                qo[there, quarter:] = -rate_odd * value_odd[:, :quarter]
            qe[...] = dot_table(qe[...], dft[4], dft[5])
            qo[...] = dot_table(qo[...], dft[6], dft[7])
            for side in range(2):
                columns = slice(side * half, (side + 1) * half)
                value = jnp.zeros((chunk, half), jnp.float32)
                product = jnp.ones((chunk, half), jnp.float32)
                for k in range(planes):
                    here = slice(k * chunk, (k + 1) * chunk)
                    there = slice((planes + k) * chunk, (planes + k + 1) * chunk)
                    if side == 0:
                        smooth, slope = qe[here, :] + qo[here, :], qe[there, :] + qo[there, :]
                    else:
                        smooth, slope = qe[here, :] - qo[here, :], qe[there, :] - qo[there, :]
                    courant = CZ * rate_ref[k, rows, columns]
                    inverse = 1.0 / (1.0 + courant)
                    factor = courant * inverse
                    value = inverse * (smooth - swirl_ref[k, rows, columns] * slope) + factor * value
                    product = factor * product
                    part[k, :, columns] = value
                    decay[k, :, columns] = product

            @pl.when(has_behind)
            def _():
                relay_copy(s, c).wait_recv()

            last = planes - 1
            entering = inc[s, rows, :]
            result[last, rows, :] = part[last] + decay[last] * entering

            @pl.when(has_ahead)
            def _():
                relay_copy(s, c).start()

            for k in range(last):
                result[k, rows, :] = part[k] + decay[k] * entering
            if s + 1 < SUBSTEPS:
                solve_chunk(s + 1, c)

                @pl.when(c < early[s + 1])
                def _():
                    start_halo(s + 1, c)

        loop(finish_rows)

    for s in range(SUBSTEPS):

        def finish(c):
            @pl.when(has_ahead)
            def _():
                halo_copy(s, 0, c).wait_send()
                relay_copy(s, c).wait_send()

            @pl.when(has_behind)
            def _():
                halo_copy(s, 1, c).wait_send()

        loop(finish)

        @pl.when(has_ahead)
        def _():
            side_copy(s, 0).wait_send()

        @pl.when(has_behind)
        def _():
            side_copy(s, 1).wait_send()

        for i in range(1, n_xs):
            bound_copy(s, i, xs).wait_send()


def solution(mesh):
    n_ax, n_xs = mesh.shape["ax"], mesh.shape["xs"]

    def body(scalar, axial_rate, swirl_rate):
        planes, rows, points = scalar.shape
        cells = rows * n_xs
        chunk = min(CHUNK, rows)
        chunks = rows // chunk
        half = points // 2
        local, spikes, mix = chunk_tables(cells, n_xs, chunk)
        even, odd, damp, rates = azimuth_tables(points, cells, n_xs)
        pairs = [split_table(x) for x in (even, odd, even.T, odd.T)]
        dft = np.stack([x for pair in pairs for x in pair])
        blocks = np.stack([np.kron(np.eye(planes), x) for x in local])
        blocks = np.concatenate(split_table(blocks), axis=1)
        blocks = blocks.reshape((n_xs, chunks) + blocks.shape[1:])
        spikes = np.pad(spikes, ((0, 0), (0, 0), (0, 126))).astype(np.float32)
        tables = [dft, blocks, spikes, damp.astype(np.float32), rates.astype(np.float32)]
        f32 = jnp.float32
        block = pltpu.VMEM((planes, rows, points), f32)
        part = pltpu.VMEM((planes, chunk, points), f32)
        pair = pltpu.VMEM((2 * planes * chunk, half), f32)
        dma = pltpu.SemaphoreType.DMA
        return pl.pallas_call(
            functools.partial(kernel, n_ax, n_xs),
            out_shape=jax.ShapeDtypeStruct(scalar.shape, f32),
            in_specs=[pl.BlockSpec(memory_space=pl.ANY)] * (3 + len(tables))
            + [pl.BlockSpec(memory_space=pltpu.SMEM)],
            out_specs=pl.BlockSpec(memory_space=pltpu.VMEM),
            scratch_shapes=[
                block, block, block,
                pltpu.VMEM(dft.shape, jnp.bfloat16),
                pltpu.VMEM(blocks.shape[1:], jnp.bfloat16),
                pltpu.VMEM(spikes.shape[1:], f32),
                pltpu.VMEM(damp.shape[1:], f32),
                pltpu.VMEM(rates.shape, f32),
                pltpu.VMEM((SUBSTEPS, 2, HALO, rows, points), f32),
                pltpu.VMEM((SUBSTEPS, rows, points), f32),
                pltpu.VMEM((SUBSTEPS, n_xs, 2 * planes, points), f32),
                pltpu.VMEM((SUBSTEPS, planes, rows, points), f32),
                part, part,
                pltpu.VMEM((planes * chunk, points), f32),
                pair, pair,
                pltpu.VMEM((2 * chunks + 2, planes, points), f32),
                pltpu.VMEM((chunks, 2, planes, points), f32),
                pltpu.VMEM((SUBSTEPS, 2, chunks, 2 * HALO, points), f32),
                pltpu.VMEM((SUBSTEPS, 2, chunks, 2 * HALO, points), f32),
                pltpu.VMEM((2, planes + 2 * HALO, points), f32),
                dma((8,)),
                dma((SUBSTEPS, 2, chunks)), dma((SUBSTEPS, 2, chunks)),
                dma((SUBSTEPS, 2)), dma((SUBSTEPS, 2)),
                dma((SUBSTEPS, chunks)), dma((SUBSTEPS, chunks)),
                dma((SUBSTEPS, n_xs - 1)), dma((SUBSTEPS, n_xs - 1)),
            ],
            compiler_params=pltpu.CompilerParams(
                collective_id=0, has_side_effects=True, vmem_limit_bytes=62 * 2**20
            ),
        )(
            scalar, axial_rate, swirl_rate,
            *[jnp.asarray(t) for t in tables],
            jnp.asarray(mix.reshape(-1).astype(np.float32)),
        )

    return jax.shard_map(
        body,
        mesh=mesh,
        in_specs=(P("ax", "xs", None), P("ax", "xs", None), P("ax", "xs", None)),
        out_specs=P("ax", "xs", None),
        check_vma=False,
    )
```

```python
import functools
import math

import jax
import jax.numpy as jnp
import ml_dtypes
import numpy as np
from jax import lax
from jax.experimental import pallas as pl
from jax.experimental.pallas import tpu as pltpu
from jax.sharding import PartitionSpec as P

CZ = 8
SUBSTEPS = 2
HALO = 4
CHUNK = 16
MESH = pl.DeviceIdType.MESH

axial_weight = 0.2
azimuth_damp = 0.5
diffusion_number = 1.0
stencil_coeffs = (
    -205.0 / 72.0,
    1.6,
    -0.2,
    8.0 / 315.0,
    -1.0 / 560.0,
)


def split_table(table):
    high = table.astype(np.float32).astype(ml_dtypes.bfloat16)
    low = (table - high.astype(np.float64)).astype(np.float32).astype(ml_dtypes.bfloat16)
    return high, low


def radial_tables(cells, groups):
    rows = cells // groups
    index = np.arange(cells, dtype=np.float64)
    radius = index + 0.5
    upper = np.where(index < cells - 1, index + 1.0, 0.0)
    sub = -diffusion_number * index / radius
    sup = -diffusion_number * upper / radius
    full = np.diag(1.0 - sub - sup) + np.diag(sub[1:], -1) + np.diag(sup[:-1], 1)
    local = np.zeros((groups, rows, rows))
    spikes = np.zeros((groups, rows, 2))
    coupling = np.zeros((2 * groups, 2 * groups))
    for d in range(groups):
        first, last = d * rows, (d + 1) * rows - 1
        local[d] = np.linalg.inv(full[first : last + 1, first : last + 1])
        if d > 0:
            spikes[d, :, 0] = -local[d][:, 0] * sub[first]
            coupling[2 * d, 2 * d - 1] = spikes[d, 0, 0]
            coupling[2 * d + 1, 2 * d - 1] = spikes[d, -1, 0]
        if d < groups - 1:
            spikes[d, :, 1] = -local[d][:, -1] * sup[last]
            coupling[2 * d, 2 * d + 2] = spikes[d, 0, 1]
            coupling[2 * d + 1, 2 * d + 2] = spikes[d, -1, 1]
    reduced = np.linalg.inv(np.eye(2 * groups) - coupling)
    mix = np.zeros((groups, 2, 2 * groups))
    for d in range(groups):
        if d > 0:
            mix[d, 0] = reduced[2 * d - 1]
        if d < groups - 1:
            mix[d, 1] = reduced[2 * d + 2]
    return local, spikes, mix


def chunk_tables(cells, groups, chunk):
    rows = cells // groups
    chunks = rows // chunk
    edges = 2 * chunks
    local, spikes, _ = radial_tables(cells, groups * chunks)
    _, outer, mix = radial_tables(cells, groups)
    weights = []
    for d in range(groups):
        coupling = np.zeros((edges, edges))
        for c in range(chunks):
            spike = spikes[d * chunks + c]
            for side, row in ((0, 0), (1, -1)):
                if c > 0:
                    coupling[2 * c + side, 2 * c - 1] = spike[row, 0]
                if c < chunks - 1:
                    coupling[2 * c + side, 2 * c + 2] = spike[row, 1]
        inner = np.linalg.inv(np.eye(edges) - coupling)
        near = np.zeros((edges, edges + 2))
        for c in range(chunks):
            if c > 0:
                near[2 * c, :edges] = inner[2 * c - 1]
                near[2 * c, edges:] = outer[d, c * chunk - 1]
            else:
                near[0, edges] = 1.0
            if c < chunks - 1:
                near[2 * c + 1, :edges] = inner[2 * c + 2]
                near[2 * c + 1, edges:] = outer[d, (c + 1) * chunk]
            else:
                near[2 * c + 1, edges + 1] = 1.0
        ends = inner[[0, -1]]
        weights.append(np.concatenate([ends.reshape(-1), mix[d].reshape(-1), near.reshape(-1)]))
    return local, spikes.reshape(groups, rows, 2), np.stack(weights)


def azimuth_tables(points, cells, groups):
    half, quarter = points // 2, points // 4
    grid = np.arange(half)
    even, odd = 2 * np.arange(quarter), 2 * np.arange(quarter) + 1

    def angle(m):
        return (grid[:, None] * m[None, :] % points) * (2.0 * math.pi / points)

    sine_even = np.sin(angle(even))
    sine_even[:, 0] = np.cos(math.pi * grid)
    table_even = np.concatenate([np.cos(angle(even)), sine_even], axis=1)
    table_odd = np.concatenate([np.cos(angle(odd)), np.sin(angle(odd))], axis=1)
    sine_m = even.copy()
    sine_m[0] = half
    wave = np.concatenate([even, sine_m, odd, odd]).astype(np.float64)
    weight = np.where((wave == 0) | (wave == half), 1.0, 2.0) / points
    radius = np.arange(cells) + 0.5
    damp = weight / (1.0 + azimuth_damp * wave[None, :] ** 2 / radius[:, None] ** 2)
    rate_even = np.where(even > 0, even, 0) * (2.0 * math.pi / points)
    rate_odd = odd * (2.0 * math.pi / points)
    rates = np.broadcast_to(np.concatenate([rate_even, rate_odd]), (8, half))
    return table_even, table_odd, damp.reshape(groups, cells // groups, points), rates


def dot(a, b):
    return jnp.dot(a, b, preferred_element_type=jnp.float32)


def split(x):
    high = x.astype(jnp.bfloat16)
    return high, (x - high.astype(jnp.float32)).astype(jnp.bfloat16)


def dot_table(x, high_table, low_table):
    rows = x.shape[0]
    high, low = split(x)
    both = dot(jnp.concatenate([high, low], axis=0), high_table)
    return both[:rows] + (both[rows:] + dot(high, low_table))


def kernel(
    n_ax, n_xs,
    u_hbm, rate_hbm, swirl_hbm, dft_hbm, local_hbm, spikes_hbm, damp_hbm, rates_hbm, mix,
    out_ref,
    field, rate_ref, swirl_ref, dft, local, spikes, damp, rates,
    halo, inc, bound, solved, part, decay, lines, qe, qo, corr, edge, pack, side_halo, extended,
    load_sem, halo_send, halo_recv, side_send, side_recv, inc_send, inc_recv, bound_send, bound_recv,
):
    planes, rows_all, points = field.shape
    half, quarter = points // 2, points // 4
    chunk = min(CHUNK, rows_all)
    chunks = rows_all // chunk
    ax, xs = lax.axis_index("ax"), lax.axis_index("xs")
    ahead, behind = lax.rem(ax + 1, n_ax), lax.rem(ax + n_ax - 1, n_ax)
    has_behind, has_ahead = ax > 0, ax < n_ax - 1

    loads = [
        pltpu.make_async_copy(source, target, load_sem.at[i])
        for i, (source, target) in enumerate(
            [
                (u_hbm, field),
                (local_hbm.at[xs], local),
                (spikes_hbm.at[xs], spikes),
                (dft_hbm, dft),
                (damp_hbm.at[xs], damp),
                (rates_hbm, rates),
                (swirl_hbm, swirl_ref),
                (rate_hbm, rate_ref),
            ]
        )
    ]
    for load in loads:
        load.start()

    barrier = pltpu.get_barrier_semaphore()

    @pl.when(has_behind)
    def _():
        pl.semaphore_signal(barrier, inc=1, device_id=(behind, xs), device_id_type=MESH)

    @pl.when(has_ahead)
    def _():
        pl.semaphore_signal(barrier, inc=1, device_id=(ahead, xs), device_id_type=MESH)

    for i in range(1, n_xs):
        pl.semaphore_signal(
            barrier, inc=1, device_id=(ax, lax.rem(xs + i, n_xs)), device_id_type=MESH
        )
    peers = n_xs - 1 + has_behind.astype(jnp.int32) + has_ahead.astype(jnp.int32)

    def rows_of(c):
        return pl.ds(pl.multiple_of(c * chunk, chunk), chunk)

    def halo_copy(s, side, c):
        start = planes - HALO if side == 0 else 0
        return pltpu.make_async_remote_copy(
            src_ref=solved.at[s, pl.ds(start, HALO), rows_of(c), :],
            dst_ref=halo.at[s, side, :, rows_of(c), :],
            send_sem=halo_send.at[s, side, c],
            recv_sem=halo_recv.at[s, side, c],
            device_id=(ahead if side == 0 else behind, xs),
            device_id_type=MESH,
        )

    def start_halo(s, c):
        @pl.when(has_ahead)
        def _():
            halo_copy(s, 0, c).start()

        @pl.when(has_behind)
        def _():
            halo_copy(s, 1, c).start()

    def side_copy(s, side):
        return pltpu.make_async_remote_copy(
            src_ref=pack.at[s, side],
            dst_ref=side_halo.at[s, side],
            send_sem=side_send.at[s, side],
            recv_sem=side_recv.at[s, side],
            device_id=(ahead if side == 0 else behind, xs),
            device_id_type=MESH,
        )

    def relay_copy(s, c):
        source = field if s == 0 else out_ref
        return pltpu.make_async_remote_copy(
            src_ref=source.at[planes - 1, rows_of(c), :],
            dst_ref=inc.at[s, rows_of(c), :],
            send_sem=inc_send.at[s, c],
            recv_sem=inc_recv.at[s, c],
            device_id=(ahead, xs),
            device_id_type=MESH,
        )

    def bound_copy(s, i, owner):
        return pltpu.make_async_remote_copy(
            src_ref=bound.at[s, owner],
            dst_ref=bound.at[s, owner],
            send_sem=bound_send.at[s, i - 1],
            recv_sem=bound_recv.at[s, i - 1],
            device_id=(ax, lax.rem(xs + i, n_xs)),
            device_id_type=MESH,
        )

    def loop(body):
        lax.fori_loop(0, chunks, lambda c, carry: (body(c), carry)[1], 0)

    @pl.when(jnp.logical_not(has_behind))
    def _():
        halo[:, 0] = jnp.zeros_like(halo[:, 0])
        side_halo[:, 0] = jnp.zeros_like(side_halo[:, 0])
        inc[...] = jnp.zeros_like(inc)

    @pl.when(jnp.logical_not(has_ahead))
    def _():
        halo[:, 1] = jnp.zeros_like(halo[:, 1])
        side_halo[:, 1] = jnp.zeros_like(side_halo[:, 1])

    edges = 2 * chunks
    near_at = 2 * edges + 4 * n_xs
    stride = near_at + edges * (edges + 2)

    def solve_chunk(s, c):
        rows = rows_of(c)
        depth = planes * chunk
        for column in range(0, points, half):
            columns = slice(column, column + half)
            high, low = split(field[:, rows, columns].reshape(depth, half))
            both = dot(local[c], high)
            x = both[:depth] + (both[depth:] + dot(local[c, :depth, :], low))
            for k in range(planes):
                here = x[k * chunk : (k + 1) * chunk]
                solved[s, k, rows, columns] = here
                edge[c, 0, k : k + 1, columns] = here[:1]
                edge[c, 1, k : k + 1, columns] = here[chunk - 1 :]

    def mixed(start, terms):
        total = jnp.zeros((planes, points), jnp.float32)
        for j, term in enumerate(terms):
            total += mix[xs * stride + start + j] * term()
        return total

    def join_chunks(s):
        inner = [lambda j=j: edge[j // 2, j % 2] for j in range(edges)]
        outer = [lambda j=j: bound[s, j // 2, (j % 2) * planes : (j % 2 + 1) * planes] for j in range(2 * n_xs)]
        for side in range(2):
            bound[s, xs, side * planes : (side + 1) * planes, :] = mixed(side * edges, inner)
        if s == 0:
            pl.semaphore_wait(barrier, peers)
            lax.fori_loop(0, early[0], lambda c, carry: (start_halo(0, c), carry)[1], 0)
        for i in range(1, n_xs):
            bound_copy(s, i, xs).start()
        for i in range(1, n_xs):
            bound_copy(s, i, lax.rem(xs + n_xs - i, n_xs)).wait_recv()
        for side in range(2):
            corr[edges + side] = mixed(2 * edges + side * 2 * n_xs, outer)
        inner += [lambda: corr[edges], lambda: corr[edges + 1]]
        for c in range(chunks):
            values = []
            for side in range(2):
                j = 2 * c + side
                value = mixed(near_at + j * (edges + 2), inner)
                corr[j] = value
                values.append(value)
            pack[s, 0, c] = jnp.concatenate([x[planes - HALO :] for x in values], axis=0)
            pack[s, 1, c] = jnp.concatenate([x[:HALO] for x in values], axis=0)

        @pl.when(has_ahead)
        def _():
            side_copy(s, 0).start()

        @pl.when(has_behind)
        def _():
            side_copy(s, 1).start()

        late = min(2, chunks) if s == 0 else chunks
        lax.fori_loop(early[s], late, lambda c, carry: (start_halo(s, c), carry)[1], 0)

    early = (min(1, chunks - 1), chunks - 1)
    for load in loads[:3]:
        load.wait()
    loop(lambda c: solve_chunk(0, c))

    for s in range(SUBSTEPS):
        result = field if s == 0 else out_ref
        join_chunks(s)
        if s == 0:
            for load in loads[3:]:
                load.wait()

        @pl.when(has_behind)
        def _():
            side_copy(s, 0).wait_recv()

        @pl.when(has_ahead)
        def _():
            side_copy(s, 1).wait_recv()

        def finish_rows(c):
            rows = rows_of(c)

            @pl.when(has_behind)
            def _():
                halo_copy(s, 0, c).wait_recv()

            @pl.when(has_ahead)
            def _():
                halo_copy(s, 1, c).wait_recv()

            if s == 0:

                @pl.when(c + 2 < chunks)
                def _():
                    start_halo(s, c + 2)

            def plane(k):
                if k < 0:
                    return halo[s, 0, k + HALO, rows, :]
                if k >= planes:
                    return halo[s, 1, k - planes, rows, :]
                return solved[s, k, rows, :]

            centre = 1.0 + axial_weight * stencil_coeffs[0]
            spike = spikes[rows, :]
            for side in range(2):
                extended[side, :HALO] = side_halo[s, 0, c, side * HALO : (side + 1) * HALO]
                extended[side, HALO : HALO + planes] = corr[2 * c + side]
                extended[side, HALO + planes :] = side_halo[s, 1, c, side * HALO : (side + 1) * HALO]
            sides = []
            for side in range(2):
                total = centre * extended[side, HALO : HALO + planes]
                for d in range(1, HALO + 1):
                    total += axial_weight * stencil_coeffs[d] * (
                        extended[side, HALO - d : HALO - d + planes]
                        + extended[side, HALO + d : HALO + d + planes]
                    )
                sides.append(total)
            for k in range(planes):
                total = centre * plane(k)
                for d in range(1, HALO + 1):
                    total += axial_weight * stencil_coeffs[d] * (plane(k - d) + plane(k + d))
                total += spike[:, 0:1] * sides[0][k : k + 1] + spike[:, 1:2] * sides[1][k : k + 1]
                lines[k * chunk : (k + 1) * chunk, :] = total
            low, high = lines[:, :half], lines[:, half:]
            even = dot_table(low + high, dft[0], dft[1])
            odd = dot_table(low - high, dft[2], dft[3])
            scale = damp[rows, :]
            rate_even, rate_odd = rates[0:1, :quarter], rates[0:1, quarter:]
            for k in range(planes):
                here = slice(k * chunk, (k + 1) * chunk)
                there = slice((planes + k) * chunk, (planes + k + 1) * chunk)
                value_even = even[here] * scale[:, :half]
                value_odd = odd[here] * scale[:, half:]
                qe[here, :] = value_even
                qo[here, :] = value_odd
                qe[there, :quarter] = rate_even * value_even[:, quarter:]
                qe[there, quarter:] = -rate_even * value_even[:, :quarter]
                qo[there, :quarter] = rate_odd * value_odd[:, quarter:]
                qo[there, quarter:] = -rate_odd * value_odd[:, :quarter]
            qe[...] = dot_table(qe[...], dft[4], dft[5])
            qo[...] = dot_table(qo[...], dft[6], dft[7])
            for side in range(2):
                columns = slice(side * half, (side + 1) * half)
                value = jnp.zeros((chunk, half), jnp.float32)
                product = jnp.ones((chunk, half), jnp.float32)
                for k in range(planes):
                    here = slice(k * chunk, (k + 1) * chunk)
                    there = slice((planes + k) * chunk, (planes + k + 1) * chunk)
                    if side == 0:
                        smooth, slope = qe[here, :] + qo[here, :], qe[there, :] + qo[there, :]
                    else:
                        smooth, slope = qe[here, :] - qo[here, :], qe[there, :] - qo[there, :]
                    courant = CZ * rate_ref[k, rows, columns]
                    inverse = 1.0 / (1.0 + courant)
                    factor = courant * inverse
                    value = inverse * (smooth - swirl_ref[k, rows, columns] * slope) + factor * value
                    product = factor * product
                    part[k, :, columns] = value
                    decay[k, :, columns] = product

            @pl.when(has_behind)
            def _():
                relay_copy(s, c).wait_recv()

            last = planes - 1
            entering = inc[s, rows, :]
            result[last, rows, :] = part[last] + decay[last] * entering

            @pl.when(has_ahead)
            def _():
                relay_copy(s, c).start()

            for k in range(last):
                result[k, rows, :] = part[k] + decay[k] * entering
            if s + 1 < SUBSTEPS:
                solve_chunk(s + 1, c)

                @pl.when(c < early[s + 1])
                def _():
                    start_halo(s + 1, c)

        loop(finish_rows)

    for s in range(SUBSTEPS):

        def finish(c):
            @pl.when(has_ahead)
            def _():
                halo_copy(s, 0, c).wait_send()
                relay_copy(s, c).wait_send()

            @pl.when(has_behind)
            def _():
                halo_copy(s, 1, c).wait_send()

        loop(finish)

        @pl.when(has_ahead)
        def _():
            side_copy(s, 0).wait_send()

        @pl.when(has_behind)
        def _():
            side_copy(s, 1).wait_send()

        for i in range(1, n_xs):
            bound_copy(s, i, xs).wait_send()


def solution(mesh):
    n_ax, n_xs = mesh.shape["ax"], mesh.shape["xs"]

    def body(scalar, axial_rate, swirl_rate):
        planes, rows, points = scalar.shape
        cells = rows * n_xs
        chunk = min(CHUNK, rows)
        chunks = rows // chunk
        half = points // 2
        local, spikes, mix = chunk_tables(cells, n_xs, chunk)
        even, odd, damp, rates = azimuth_tables(points, cells, n_xs)
        pairs = [split_table(x) for x in (even, odd, even.T, odd.T)]
        dft = np.stack([x for pair in pairs for x in pair])
        blocks = np.stack([np.kron(np.eye(planes), x) for x in local])
        blocks = np.concatenate(split_table(blocks), axis=1)
        blocks = blocks.reshape((n_xs, chunks) + blocks.shape[1:])
        spikes = np.pad(spikes, ((0, 0), (0, 0), (0, 126))).astype(np.float32)
        tables = [dft, blocks, spikes, damp.astype(np.float32), rates.astype(np.float32)]
        f32 = jnp.float32
        block = pltpu.VMEM((planes, rows, points), f32)
        part = pltpu.VMEM((planes, chunk, points), f32)
        pair = pltpu.VMEM((2 * planes * chunk, half), f32)
        dma = pltpu.SemaphoreType.DMA
        return pl.pallas_call(
            functools.partial(kernel, n_ax, n_xs),
            out_shape=jax.ShapeDtypeStruct(scalar.shape, f32),
            in_specs=[pl.BlockSpec(memory_space=pl.ANY)] * (3 + len(tables))
            + [pl.BlockSpec(memory_space=pltpu.SMEM)],
            out_specs=pl.BlockSpec(memory_space=pltpu.VMEM),
            scratch_shapes=[
                block, block, block,
                pltpu.VMEM(dft.shape, jnp.bfloat16),
                pltpu.VMEM(blocks.shape[1:], jnp.bfloat16),
                pltpu.VMEM(spikes.shape[1:], f32),
                pltpu.VMEM(damp.shape[1:], f32),
                pltpu.VMEM(rates.shape, f32),
                pltpu.VMEM((SUBSTEPS, 2, HALO, rows, points), f32),
                pltpu.VMEM((SUBSTEPS, rows, points), f32),
                pltpu.VMEM((SUBSTEPS, n_xs, 2 * planes, points), f32),
                pltpu.VMEM((SUBSTEPS, planes, rows, points), f32),
                part, part,
                pltpu.VMEM((planes * chunk, points), f32),
                pair, pair,
                pltpu.VMEM((2 * chunks + 2, planes, points), f32),
                pltpu.VMEM((chunks, 2, planes, points), f32),
                pltpu.VMEM((SUBSTEPS, 2, chunks, 2 * HALO, points), f32),
                pltpu.VMEM((SUBSTEPS, 2, chunks, 2 * HALO, points), f32),
                pltpu.VMEM((2, planes + 2 * HALO, points), f32),
                dma((8,)),
                dma((SUBSTEPS, 2, chunks)), dma((SUBSTEPS, 2, chunks)),
                dma((SUBSTEPS, 2)), dma((SUBSTEPS, 2)),
                dma((SUBSTEPS, chunks)), dma((SUBSTEPS, chunks)),
                dma((SUBSTEPS, n_xs - 1)), dma((SUBSTEPS, n_xs - 1)),
            ],
            compiler_params=pltpu.CompilerParams(
                collective_id=0, has_side_effects=True, vmem_limit_bytes=62 * 2**20
            ),
        )(
            scalar, axial_rate, swirl_rate,
            *[jnp.asarray(t) for t in tables],
            jnp.asarray(mix.reshape(-1).astype(np.float32)),
        )

    return jax.shard_map(
        body,
        mesh=mesh,
        in_specs=(P("ax", "xs", None), P("ax", "xs", None), P("ax", "xs", None)),
        out_specs=P("ax", "xs", None),
        check_vma=False,
    )
```
